256 devices in a mesh: grp: 16 (over z_lo, x, core), sp: 16 (over y, z_hi).
Axes of the slice: x: 4, y: 4, z: 8 (z_hi: 4, z_lo: 2; z = z_hi * 2 + z_lo), core: 2. Of those that a mesh axis runs over, the one named last changes fastest.
Arguments:
- img_q: bfloat16 [16, 2048, 3072], P('grp', 'sp'), may hold values from -6 to 6
- img_k: bfloat16 [16, 2048, 3072], P('grp', 'sp'), may hold values from -6 to 6
- img_v: bfloat16 [16, 2048, 3072], P('grp', 'sp'), may hold values from -6 to 6
- cond_rows: bfloat16 [16, 128, 9216], P('grp', 'sp'), may hold values from -6 to 6
- prompt_len: int32 [16], replicated, may hold values from 1 to 64, 512 in all
- ref_count: int32 [16], replicated, may hold values from 1 to 64, 512 in all
- assign: int32 [16], replicated, may hold values from 0 to 15, each once
Outputs:
- img_out: bfloat16 [16, 2048, 3072], P('grp', 'sp')
- txt_out: bfloat16 [16, 128, 3072], P('grp', 'sp')
The draws below stay inside these ranges and needn't reach their ends.
Inputs may be any that keep to these rules, and one draw needn't show every extreme that they name: `prompt_len`: the 16 prompt lengths sum to 512. `ref_count`: the 16 reference token counts sum to 512. `assign`: every group serves exactly one request.
All inputs are finite; a program needn't handle non-finite values.
Results may differ from the reference program's by a relative error of at most 0.0048.
Values may be sent and summed in bfloat16 or wider, within the bound.
No kernel may reach another device: no remote copies, remote signals or barrier semaphores. Data moves between devices by JAX's collectives and lax.ppermute only.
A program may use at most 128 MiB of HBM per device.

```python
import math
import jax
import jax.numpy as jnp
import numpy as np
from jax import lax

HEADS = 24
HD = 128
D = 3072
IMG = 2048
TXT = 128
PROMPT_SLOTS = 64
REF_SLOTS = 64
N_GRP = 16


def base_field(key):
    return jnp.clip(jax.random.normal(key, (N_GRP, IMG, D), jnp.float32), -6.0, 6.0)


def draw_img_k(key, part):
    key = jax.random.fold_in(key, 1)
    field = base_field(key)
    return field.astype(jnp.bfloat16)


def draw_img_q(key, part):
    key = jax.random.fold_in(key, 2)
    field = base_field(key)
    return field.astype(jnp.bfloat16)


def steps_of(own_key, dims, cuts, smallest, high):
    gain = 1.0
    for axis_at, parts in cuts:
        draws = jax.random.uniform(jax.random.fold_in(jax.random.fold_in(own_key, 6), axis_at), (parts,), jnp.float32, smallest / len(cuts), high / len(cuts))
        gain = gain * jnp.repeat(jnp.exp(draws), dims[axis_at] // parts).reshape((-1,) + (1,) * (len(dims) - 1 - axis_at))
    return gain


def length_profile(count, total, bound, lean):
    portions = [(1 << 20) // math.isqrt(grade ** lean) + 1 for grade in range(2, count + 1)]
    surplus, given = total - bound - (count - 1), [1] * (count - 1)
    while surplus > 0:
        free = [i for i in range(count - 1) if given[i] < bound]
        pool, left = sum([portions[i] for i in free]), surplus
        for i in free:
            more = min(bound - given[i], max(1, left * portions[i] // pool), surplus)
            given[i] = given[i] + more
            surplus = surplus - more
    return np.array([bound] + given)


def ragged(stream_key, count, total, limit, skew):
    if count == 2:
        one = jax.random.randint(stream_key, (), max(1, total - limit), min(limit, total - 1) + 1)
        return jnp.stack([one, total - one])
    lengths = jnp.asarray(length_profile(count, total, limit, skew), jnp.int32)
    couples = (count - 1) // 2
    source_of, sink = lengths[1:1 + 2 * couples:2], lengths[2:2 + 2 * couples:2]
    margin = jnp.minimum(source_of - 1, limit - sink)
    moved = jax.random.randint(jax.random.fold_in(stream_key, 1), (couples,), 0, 1 << 20) % (margin + 1)
    lengths = lengths.at[1:1 + 2 * couples:2].set(source_of - moved).at[2:2 + 2 * couples:2].set(sink + moved)
    return lengths[jax.random.permutation(jax.random.fold_in(stream_key, 2), count)]


def bell_draw(own_key, extent, spread, limit, pieces=(), held_as=jnp.bfloat16):
    entries = jax.random.normal(own_key, extent, jnp.float32) * spread
    if len(pieces) > 0:
        entries = steps_of(own_key, extent, pieces, -0.22, 0.18) * entries
    return jnp.clip(entries, min=-limit, max=limit).astype(held_as)


def setup_inputs(seed: int = 0) -> dict:
    splits = jax.random.split(jax.random.key(seed), 8)
    img_q = draw_img_q(jax.random.fold_in(splits[7], 71), 0)
    img_k = draw_img_k(jax.random.fold_in(splits[7], 71), 0)
    img_v = bell_draw(splits[2], (N_GRP, IMG, D), 1.0, 6.0, ((0, 16), (1, 16)))
    cond_rows = bell_draw(splits[3], (N_GRP, TXT, 3 * D), 1.0, 6.0, ((0, 16), (1, 16)))
    prompt_len = ragged(splits[4], N_GRP, N_GRP * PROMPT_SLOTS // 2, PROMPT_SLOTS, 2).astype(jnp.int32)
    ref_count = ragged(splits[5], N_GRP, N_GRP * REF_SLOTS // 2, REF_SLOTS, 1).astype(jnp.int32)
    assign = jax.random.permutation(splits[6], N_GRP).astype(jnp.int32)
    return {"img_q": img_q, "img_k": img_k, "img_v": img_v, "cond_rows": cond_rows, "prompt_len": prompt_len, "ref_count": ref_count, "assign": assign}


NEG_FILL = -1e+30

def attend(queries, keys_all, values_all, alive):
    rows = queries.shape[0]
    query_heads = queries.astype(jnp.float32).reshape(rows, HEADS, HD)
    key_heads = keys_all.astype(jnp.float32).reshape(rows, HEADS, HD)
    value_heads = values_all.astype(jnp.float32).reshape(rows, HEADS, HD)
    scores = jnp.einsum('qhd,khd->hqk', query_heads, key_heads) * (1.0 / math.sqrt(HD))
    scores = jnp.where(alive[None, None, :], scores, NEG_FILL)
    top = lax.optimization_barrier(jnp.max(scores, axis=-1, keepdims=True))
    weights = jnp.exp(scores - top)
    totals = lax.optimization_barrier(jnp.sum(weights, axis=-1))
    rounded = lax.optimization_barrier(weights.astype(jnp.bfloat16)).astype(jnp.float32)
    mixed = jnp.einsum('hqk,khd->qhd', rounded, value_heads) / jnp.transpose(totals)[:, :, None]
    return mixed.reshape(rows, HEADS * HD)

def reference(img_q, img_k, img_v, cond_rows, prompt_len, ref_count, assign):
    order = jnp.arange(N_GRP, dtype=jnp.int32)
    slots = jnp.arange(TXT, dtype=jnp.int32)

    def one_group(group):
        owner = jnp.sum(jnp.where(assign == group, order, 0)).astype(jnp.int32)
        owner_prompt = jnp.sum(jnp.where(order == owner, prompt_len, 0))
        owner_ref = jnp.sum(jnp.where(order == owner, ref_count, 0))
        text = lax.dynamic_index_in_dim(cond_rows, owner, 0, keepdims=False)
        text_alive = jnp.where(slots < REF_SLOTS, slots < owner_ref, slots - REF_SLOTS < owner_prompt)
        image_q = lax.dynamic_index_in_dim(img_q, group, 0, keepdims=False)
        image_k = lax.dynamic_index_in_dim(img_k, group, 0, keepdims=False)
        image_v = lax.dynamic_index_in_dim(img_v, group, 0, keepdims=False)
        queries = jnp.concatenate([image_q, text[:, :D]], axis=0)
        keys_all = jnp.concatenate([image_k, text[:, D:2 * D]], axis=0)
        values_all = jnp.concatenate([image_v, text[:, 2 * D:]], axis=0)
        alive = jnp.concatenate([jnp.ones((IMG,), dtype=bool), text_alive], axis=0)
        mixed = attend(queries, keys_all, values_all, alive)
        image_out = mixed[:IMG].astype(jnp.bfloat16)
        text_out = jnp.where(text_alive[:, None], mixed[IMG:], jnp.float32(0.0)).astype(jnp.bfloat16)
        return (image_out, text_out)
    image_out, text_out = lax.map(one_group, order)
    return (image_out, text_out)
```

```python
import functools
import math

import jax
import jax.numpy as jnp
from jax import lax
from jax.experimental import pallas as pl
from jax.experimental.pallas import tpu as pltpu
from jax.sharding import PartitionSpec as P

HD = 128
NEG_FILL = -1e30
VMEM_LIMIT = 48 * 1024 * 1024


def call(body, out_shape, in_specs, out_specs, scratch_shapes=()):
    return pl.pallas_call(
        body,
        out_shape=out_shape,
        in_specs=in_specs,
        out_specs=out_specs,
        scratch_shapes=list(scratch_shapes),
        compiler_params=pltpu.CompilerParams(vmem_limit_bytes=VMEM_LIMIT),
    )


VMEM = pl.BlockSpec(memory_space=pltpu.VMEM)
SMEM = pl.BlockSpec(memory_space=pltpu.SMEM)


class Plan:
    def __init__(self, shards, rows, text_rows, width):
        self.shards = shards
        self.rows = rows
        self.half = rows // 2
        self.text_rows = text_rows
        self.width = width

    def side(self, device):
        return (device >> 2) & 1

    def shared(self, device):
        return self.shards + ((device >> 3) << 2) + (device & 3)


def head(column):
    return slice(column * HD, (column + 1) * HD)


def pack_first(plan, q, k, v, out):
    rows, half = plan.rows, plan.half
    for device in range(plan.shards):
        side, shared = plan.side(device), plan.shared(device)
        mine = slice(side * half, (side + 1) * half)
        out[device, 0:rows, :] = q[:, head(device)]
        out[device, rows : rows + half, :] = q[mine, head(shared)]
        out[device, rows + half : 2 * rows, :] = k[mine, head(shared)]
        out[device, 2 * rows : 2 * rows + half, :] = v[mine, head(shared)]


def pack_second(plan, k, v, text, out):
    rows = plan.rows
    heads = plan.width // HD
    wide = text[...].astype(jnp.float32)
    for device in range(plan.shards):
        out[device, 0:rows, :] = k[:, head(device)]
        out[device, rows : 2 * rows, :] = v[:, head(device)]
        pieces = [wide[:, head(part * heads + own)] for own in (device, plan.shared(device)) for part in range(3)]
        out[device, 2 * rows :, :] = jnp.concatenate(pieces, axis=0).astype(out.dtype)


def attend(queries, keys, values, alive, image_keys):
    factor = math.log2(math.e) / math.sqrt(HD)
    dims = (((1,), (1,)), ((), ()))
    image = lax.dot_general(queries, keys[:image_keys], dims, preferred_element_type=jnp.float32)
    text = lax.dot_general(queries, keys[image_keys:], dims, preferred_element_type=jnp.float32)
    text = jnp.where(alive, text, NEG_FILL)
    top = jnp.maximum(jnp.max(image, axis=1, keepdims=True), jnp.max(text, axis=1, keepdims=True))
    image = jnp.exp2((image - top) * factor).astype(jnp.bfloat16)
    text = jnp.exp2((text - top) * factor).astype(jnp.bfloat16)
    mixed = jnp.dot(image, values[:image_keys], preferred_element_type=jnp.float32)
    mixed = mixed + jnp.dot(text, values[image_keys:], preferred_element_type=jnp.float32)
    return (mixed[:, :HD] / mixed[:, HD:]).astype(jnp.bfloat16)


def owner_counts(group, assign, prompt_len, ref_count, groups):
    prompt, ref = prompt_len[0], ref_count[0]
    for request in range(1, groups):
        here = assign[request] == group
        prompt = jnp.where(here, prompt_len[request], prompt)
        ref = jnp.where(here, ref_count[request], ref)
    return prompt, ref


def attention(plan, groups, place, assign, prompt_len, ref_count, first, second, swapped, out, k_own, v_own, k_shared, v_shared, texts):
    rows, half, shards, text_rows = plan.rows, plan.half, plan.shards, plan.text_rows
    images = shards * rows
    slots = shards * text_rows
    prompt, ref = owner_counts(place[0], assign, prompt_len, ref_count, groups)
    ref_slots = slots - slots // 2
    slot = lax.broadcasted_iota(jnp.int32, (1, slots), 1)
    alive = slot < jnp.where(slot < ref_slots, ref, ref_slots + prompt)

    for values in (v_own, v_shared):
        values[:, HD:] = jnp.ones((images + slots, HD), jnp.bfloat16)
    for source in range(shards):
        at = source * rows
        k_own[at : at + rows, :] = second[source, 0:rows, :]
        v_own[at : at + rows, :HD] = second[source, rows : 2 * rows, :]
        mid = at + half
        k_shared[at:mid, :] = first[source, rows + half : 2 * rows, :]
        v_shared[at:mid, :HD] = first[source, 2 * rows : 2 * rows + half, :]
        k_shared[mid : at + rows, :] = swapped[source, 0:half, :]
        v_shared[mid : at + rows, :HD] = swapped[source, half : 2 * half, :]
    for source in range(0, shards, 2):
        one = second[source, 2 * rows :, :].astype(jnp.float32)
        two = second[source + 1, 2 * rows :, :].astype(jnp.float32)
        at = source * text_rows
        for part in range(6):
            cut = slice(part * text_rows, (part + 1) * text_rows)
            both = jnp.concatenate([one[cut], two[cut]], axis=0).astype(jnp.bfloat16)
            place_at = slice(at, at + 2 * text_rows)
            into = slice(images + at, images + at + 2 * text_rows)
            if part == 0:
                texts[0, place_at, :] = both
            elif part == 1:
                k_own[into, :] = both
            elif part == 2:
                v_own[into, :HD] = both
            elif part == 3:
                texts[1, place_at, :] = both
            elif part == 4:
                k_shared[into, :] = both
            else:
                v_shared[into, :HD] = both

    def own_block(step, carry):
        source = step * 2
        queries = first[pl.ds(source, 2), 0:rows, :].reshape(2 * rows, HD)
        mixed = attend(queries, k_own, v_own, alive, images)
        out[pl.ds(source, 2), 0:rows, :] = mixed.reshape(2, rows, HD)
        return carry

    def shared_block(step, carry):
        source = step * 4
        queries = first[pl.ds(source, 4), rows : rows + half, :].reshape(4 * half, HD)
        mixed = attend(queries, k_shared, v_shared, alive, images)
        out[pl.ds(source, 4), rows : rows + half, :] = mixed.reshape(4, half, HD)
        return carry

    lax.fori_loop(0, shards // 2, own_block, 0, unroll=2)
    lax.fori_loop(0, shards // 4, shared_block, 0, unroll=2)
    own_text = attend(texts[0], k_own, v_own, alive, images).astype(jnp.float32)
    shared_text = attend(texts[1], k_shared, v_shared, alive, images).astype(jnp.float32)
    for source in range(shards):
        cut = slice(source * text_rows, (source + 1) * text_rows)
        out[source, rows + half :, :] = jnp.concatenate([own_text[cut], shared_text[cut]], axis=0).astype(jnp.bfloat16)


def unpack(plan, groups, place, assign, prompt_len, ref_count, returned, image_out, text_out):
    rows, half, shards, text_rows = plan.rows, plan.half, plan.shards, plan.text_rows
    slots = shards * text_rows
    prompt, ref = owner_counts(place[0], assign, prompt_len, ref_count, groups)
    ref_slots = slots - slots // 2
    slot = place[1] * text_rows + lax.broadcasted_iota(jnp.int32, (text_rows, 1), 0)
    alive = slot < jnp.where(slot < ref_slots, ref, ref_slots + prompt)
    for device in range(shards):
        side, shared = plan.side(device), plan.shared(device)
        image_out[:, head(device)] = returned[device, 0:rows, :]
        image_out[side * half : (side + 1) * half, head(shared)] = returned[device, rows : rows + half, :]
        text = returned[device, rows + half :, :].astype(jnp.float32)
        text_out[:, head(device)] = jnp.where(alive, text[:text_rows], 0.0).astype(text_out.dtype)
        if side == 0:
            text_out[:, head(shared)] = jnp.where(alive, text[text_rows:], 0.0).astype(text_out.dtype)


def route(cond, group, assign, groups):
    order = jnp.arange(groups, dtype=jnp.int32)

    def exchange(data, bit):
        return lax.ppermute(data, "grp", [(i, i ^ bit) for i in range(groups)])

    def target(source):
        return jnp.sum(jnp.where(order == source, assign, 0))

    held = [cond, exchange(cond, 8)]
    other = exchange(jnp.stack(held), 1)
    held = held + [other[0], other[1]]
    targets = [target(group ^ bits) for bits in (0, 8, 1, 9)]

    def bound_for(place):
        total = jnp.zeros_like(cond)
        for packet, aim in zip(held, targets):
            total = jnp.where(aim == place, packet, total)
        return total

    came = exchange(jnp.stack([bound_for(group ^ 2), bound_for(group ^ 6)]), 2)
    mine = bound_for(group) + came[0]
    across = bound_for(group ^ 4) + came[1]
    return mine + exchange(across, 4)


def on_device(img_q, img_k, img_v, cond_rows, prompt_len, ref_count, assign):
    group = lax.axis_index("grp")
    shard = lax.axis_index("sp")
    groups = lax.axis_size("grp")
    shards = lax.axis_size("sp")
    _, rows, width = img_q.shape
    text_rows = cond_rows.shape[1]
    half = rows // 2
    plan = Plan(shards, rows, text_rows, width)
    place = jnp.stack([group, shard]).astype(jnp.int32)
    dtype = img_q.dtype

    def across(data):
        return lax.all_to_all(data, "sp", split_axis=0, concat_axis=0, tiled=True)

    text = route(cond_rows[0], group, assign, groups)
    first = call(
        functools.partial(pack_first, plan),
        jax.ShapeDtypeStruct((shards, 2 * rows + half, HD), dtype),
        [VMEM] * 3,
        VMEM,
    )(img_q[0], img_k[0], img_v[0])
    first = across(first)
    second = call(
        functools.partial(pack_second, plan),
        jax.ShapeDtypeStruct((shards, 2 * rows + 6 * text_rows, HD), dtype),
        [VMEM] * 3,
        VMEM,
    )(img_k[0], img_v[0], text)
    second = across(second)
    swapped = lax.ppermute(first[:, rows + half :, :], "sp", [(i, i ^ 4) for i in range(shards)])
    total = shards * (rows + text_rows)
    mixed = call(
        functools.partial(attention, plan, groups),
        jax.ShapeDtypeStruct((shards, rows + half + 2 * text_rows, HD), dtype),
        [SMEM] * 4 + [VMEM] * 3,
        VMEM,
        [
            pltpu.VMEM((total, HD), dtype),
            pltpu.VMEM((total, 2 * HD), dtype),
            pltpu.VMEM((total, HD), dtype),
            pltpu.VMEM((total, 2 * HD), dtype),
            pltpu.VMEM((2, shards * text_rows, HD), dtype),
        ],
    )(place, assign, prompt_len, ref_count, first, second, swapped)
    returned = across(mixed)
    image_out, text_out = call(
        functools.partial(unpack, plan, groups),
        (
            jax.ShapeDtypeStruct((rows, width), dtype),
            jax.ShapeDtypeStruct((text_rows, width), dtype),
        ),
        [SMEM] * 4 + [VMEM],
        (VMEM, VMEM),
    )(place, assign, prompt_len, ref_count, returned)
    return (image_out[None], text_out[None])


def solution(mesh):
    spec = P("grp", "sp", None)
    return jax.shard_map(
        on_device,
        mesh=mesh,
        in_specs=(spec, spec, spec, spec, P(), P(), P()),
        out_specs=(spec, spec),
        check_vma=False,
    )
```

```python
import functools
import math

import jax
import jax.numpy as jnp
from jax import lax
from jax.experimental import pallas as pl
from jax.experimental.pallas import tpu as pltpu
from jax.sharding import PartitionSpec as P

HD = 128
SIDE = 4
NEG_FILL = -1e30
FLOPS_S = 30000000000
KEY_SPAN = 512
FACTOR = math.log2(math.e) / math.sqrt(HD)
VMEM_LIMIT = 48 * 1024 * 1024
VMEM = pl.BlockSpec(memory_space=pltpu.VMEM)
SMEM = pl.BlockSpec(memory_space=pltpu.SMEM)
HBM = pl.BlockSpec(memory_space=pltpu.HBM)


def call(body, out_shape, in_specs, out_specs, scratch_shapes=(), grid=(), cost=None):
    return pl.pallas_call(
        body,
        grid=grid,
        cost_estimate=cost,
        out_shape=out_shape,
        in_specs=in_specs,
        out_specs=out_specs,
        scratch_shapes=list(scratch_shapes),
        compiler_params=pltpu.CompilerParams(vmem_limit_bytes=VMEM_LIMIT),
    )


class Plan:
    def __init__(self, groups, shards, rows, text_rows, width):
        self.groups = groups
        self.shards = shards
        self.rows = rows
        self.half = rows // 2
        self.text_rows = text_rows
        self.heads = width // HD
        self.slots = shards * text_rows
        self.images = shards * rows

    def side(self, device):
        return (device // SIDE) % 2

    def shared(self, device):
        return self.shards + (device // SIDE // 2) * SIDE + device % SIDE


def head(column):
    return slice(column * HD, (column + 1) * HD)


def head_at(column):
    return pl.ds(pl.multiple_of(column * HD, HD), HD)


def step_to(place, dy, dz):
    return lax.rem(place[1] + dy, SIDE), lax.rem(place[2] + dz, SIDE)


def step_from(place, dy, dz):
    y, z = step_to(place, SIDE - dy, SIDE - dz)
    return y * SIDE + z


def fetch(refs, columns, held, sems):
    copies = [pltpu.make_async_copy(ref.at[:, columns], held.at[part], sems.at[part]) for part, ref in enumerate(refs)]
    for copy in copies:
        copy.start()
    for copy in copies:
        copy.wait()


def pack_shared(plan, place, q, k, v, *rest):
    rows, first = plan.rows, plan.shards * HD
    outs, (held, sems) = rest[:SIDE], rest[SIDE:]
    fetch((q, k, v), slice(first, plan.heads * HD), held, sems)
    for dz in range(SIDE):
        z = lax.rem(place[2] + dz, SIDE)
        for pair in range(2):
            for part in range(3):
                outs[dz][pair, part * rows : (part + 1) * rows, :] = held[part, :, head_at(pair * SIDE + z)]


def pack_whole(plan, place, assign, q, k, v, h0, h2, h4, h6, early, out):
    rows = plan.rows
    owner = jnp.int32(0)
    for request in range(1, plan.groups):
        owner = jnp.where(assign[request] == place[0], request, owner)
    came = lax.rem(lax.div(lax.bitwise_xor(owner, place[0]), 2), 4)
    for device in range(plan.shards):
        for part, ref in enumerate((q, k, v)):
            out[device, part * rows : (part + 1) * rows, :] = ref[:, head(device)]
        pieces = []
        for own in (device, plan.shared(device)):
            for part in range(3):
                at = head(part * plan.heads + own)
                low = jnp.where(came == 0, h0[:, at].astype(jnp.float32), h2[:, at].astype(jnp.float32))
                high = jnp.where(came == 2, h4[:, at].astype(jnp.float32), h6[:, at].astype(jnp.float32))
                pieces.append(jnp.where(came < 2, low, high))
        out[device, 3 * rows :, :] = jnp.concatenate(pieces, axis=0).astype(jnp.bfloat16)


def choose(place, assign, h0, h8, h1, h9, *outs):
    group = place[0]
    for turn, out in zip((0, 2, 4, 6), outs):
        target = lax.bitwise_xor(group, turn)
        out[...] = h0[...]
        for bits, ref in ((1, h1), (8, h8), (9, h9)):

            @pl.when(assign[lax.bitwise_xor(group, bits)] == target)
            def _(ref=ref, out=out):
                out[...] = ref[...]


def regroup_shared(plan, place, *refs):
    rows, half = plan.rows, plan.half
    ins, outs = refs[:SIDE], refs[SIDE:]
    for dy in range(SIDE):
        y = lax.rem(place[1] + dy, SIDE)
        pair, side = lax.div(y, 2), lax.rem(y, 2)
        mine = pl.ds(pl.multiple_of(side * half, half), half)
        for dz in range(SIDE):
            outs[dy][dz, 0:half, :] = ins[dz][pair, mine, :]
            outs[dy][dz, half:, :] = ins[dz][pair, rows:, :]


def owner_counts(plan, place, assign, prompt_len, ref_count):
    prompt, ref = prompt_len[0], ref_count[0]
    for request in range(1, plan.groups):
        here = assign[request] == place[0]
        prompt = jnp.where(here, prompt_len[request], prompt)
        ref = jnp.where(here, ref_count[request], ref)
    return prompt, ref


def is_alive(plan, slot, counts):
    prompt, ref = counts
    ref_slots = plan.slots - plan.slots // 2
    return slot < jnp.where(slot < ref_slots, ref, ref_slots + prompt)


def scores(queries, keys):
    return lax.dot_general(queries, keys, (((1,), (1,)), ((), ())), preferred_element_type=jnp.float32)


def weights(score, top):
    return jnp.exp2((score - top) * FACTOR).astype(jnp.bfloat16)


def largest(score):
    return jnp.max(score, axis=1, keepdims=True)


def total(weight, values):
    return jnp.dot(weight, values, preferred_element_type=jnp.float32)


def attend(queries, pieces):
    mixed = top = None
    for keys, values, alive in pieces:
        score = scores(queries, keys)
        if alive is not None:
            score = jnp.where(alive, score, NEG_FILL)
        higher = largest(score)
        if top is not None:
            higher = jnp.maximum(top, higher)
        part = total(weights(score, higher), values)
        mixed = part if top is None else mixed * jnp.exp2((top - higher) * FACTOR) + part
        top = higher
    return (mixed[:, :HD] / mixed[:, HD:]).astype(jnp.bfloat16)


def attention(plan, place, assign, prompt_len, ref_count, came, p0, p1, p2, p3, out, keys, values, texts, text_values):
    rows, half, images, text_rows, slots = plan.rows, plan.half, plan.images, plan.text_rows, plan.slots
    alive = is_alive(plan, lax.broadcasted_iota(jnp.int32, (1, slots), 1), owner_counts(plan, place, assign, prompt_len, ref_count))
    parts = (p0, p1, p2, p3)
    for source in range(0, plan.shards, 2):
        pair = [came[source + i, 3 * rows :, :].astype(jnp.float32) for i in range(2)]
        at = source * text_rows
        for kind in range(6):
            cut = slice(kind * text_rows, (kind + 1) * text_rows)
            both = jnp.concatenate([one[cut] for one in pair], axis=0).astype(jnp.bfloat16)
            if kind in (2, 5):
                text_values[kind // 3, at : at + 2 * text_rows, :HD] = both
            else:
                texts[kind, at : at + 2 * text_rows, :] = both
    text_values[:, :, HD:] = jnp.ones((2, slots, HD), jnp.bfloat16)
    for source in range(plan.shards):
        at = slice(source * rows, (source + 1) * rows)
        keys[0, at, :] = came[source, rows : 2 * rows, :]
        values[0, at, :HD] = came[source, 2 * rows : 3 * rows, :]
        part, dz = parts[source // SIDE], source % SIDE
        keys[1, at, :] = part[dz, half : half + rows, :]
        values[1, at, :HD] = part[dz, half + rows :, :]
    values[:, :, HD:] = jnp.ones((2, images, HD), jnp.bfloat16)

    def mix(which, queries):
        cuts = [slice(at, at + KEY_SPAN) for at in range(0, images, KEY_SPAN)]
        pieces = [(keys[which, cut, :], values[which, cut, :], None) for cut in cuts]
        return attend(queries, pieces + [(texts[3 * which + 1], text_values[which], alive)])

    for source in range(0, plan.shards, 2):
        mixed = mix(0, came[source : source + 2, 0:rows, :].reshape(2 * rows, HD))
        out[source : source + 2, 0:rows, :] = mixed.reshape(2, rows, HD)
    for dy in range(SIDE):
        mixed = mix(1, parts[dy][:, 0:half, :].reshape(SIDE * half, HD))
        for dz in range(SIDE):
            out[step_from(place, dy, dz), rows : rows + half, :] = mixed[dz * half : (dz + 1) * half]
    own_text, other_text = (mix(which, texts[3 * which]).astype(jnp.float32) for which in range(2))
    for source in range(plan.shards):
        cut = slice(source * text_rows, (source + 1) * text_rows)
        out[source, rows + half :, :] = jnp.concatenate([own_text[cut], other_text[cut]], axis=0).astype(jnp.bfloat16)


def unpack(plan, place, assign, prompt_len, ref_count, returned, image_out, text_out):
    rows, half, text_rows = plan.rows, plan.half, plan.text_rows
    slot = (place[1] * SIDE + place[2]) * text_rows + lax.broadcasted_iota(jnp.int32, (text_rows, 1), 0)
    alive = is_alive(plan, slot, owner_counts(plan, place, assign, prompt_len, ref_count))
    for device in range(plan.shards):
        side, shared = plan.side(device), plan.shared(device)
        image_out[:, head(device)] = returned[device, 0:rows, :]
        image_out[side * half : (side + 1) * half, head(shared)] = returned[device, rows : rows + half, :]
        text = returned[device, rows + half :, :].astype(jnp.float32)
        text_out[:, head(device)] = jnp.where(alive, text[:text_rows], 0.0).astype(text_out.dtype)
        if side == 0:
            text_out[:, head(shared)] = jnp.where(alive, text[text_rows:], 0.0).astype(text_out.dtype)


def route(plan, place, assign, rows):
    def exchange(data, bits):
        return lax.ppermute(data, "grp", [(i, i ^ bits) for i in range(plan.groups)])

    held = [rows] + [exchange(rows, bits) for bits in (8, 1, 9)]
    shape = jax.ShapeDtypeStruct(rows.shape, rows.dtype)
    bound = call(choose, (shape,) * 4, [SMEM] * 2 + [VMEM] * 4, (VMEM,) * 4)(place, assign, *held)
    return [bound[0]] + [exchange(packet, bits) for packet, bits in zip(bound[1:], (2, 4, 6))]


def shift(data, dy, dz, shards):
    pairs = [(i, (i // SIDE + dy) % SIDE * SIDE + (i + dz) % SIDE) for i in range(shards)]
    return lax.ppermute(data, "sp", pairs)


def along_z(parts, shards):
    return [parts[0]] + [shift(parts[dz], 0, dz, shards) for dz in range(1, SIDE)]


def along_y(parts, shards):
    return [parts[0]] + [shift(parts[dy], dy, 0, shards) for dy in range(1, SIDE)]


def on_device(img_q, img_k, img_v, cond_rows, prompt_len, ref_count, assign):
    group = lax.axis_index("grp")
    shard = lax.axis_index("sp")
    groups = lax.axis_size("grp")
    shards = lax.axis_size("sp")
    _, rows, width = img_q.shape
    text_rows = cond_rows.shape[1]
    half = rows // 2
    plan = Plan(groups, shards, rows, text_rows, width)
    place = jnp.stack([group, shard // SIDE, shard % SIDE]).astype(jnp.int32)
    dtype = img_q.dtype

    def like(*shape, dtype=dtype):
        return jax.ShapeDtypeStruct(shape, dtype)

    images = (img_q[0], img_k[0], img_v[0])
    shared = width - shards * HD
    parts = call(
        functools.partial(pack_shared, plan),
        (like(2, 3 * rows, HD),) * SIDE,
        [SMEM] + [HBM] * 3,
        (VMEM,) * SIDE,
        [pltpu.VMEM((3, rows, shared), dtype), pltpu.SemaphoreType.DMA((3,))],
    )(place, *images)
    parts = along_z(parts, shards)
    early = parts[1]
    parts = call(
        functools.partial(regroup_shared, plan),
        (like(SIDE, half + 2 * rows, HD),) * SIDE,
        [SMEM] + [VMEM] * SIDE,
        (VMEM,) * SIDE,
        cost=pl.CostEstimate(flops=FLOPS_S, transcendentals=0, bytes_accessed=0),
    )(place, *parts)
    parts = along_y(parts, shards)

    texts = route(plan, place, assign, cond_rows[0])
    whole = call(
        functools.partial(pack_whole, plan),
        like(shards, 3 * rows + 6 * text_rows, HD),
        [SMEM] * 2 + [VMEM] * 7 + [pl.BlockSpec(memory_space=pl.ANY)],
        VMEM,
    )(place, assign, *images, *texts, early)
    whole = lax.all_to_all(whole, "sp", split_axis=0, concat_axis=0, tiled=True)

    lengths = (assign, prompt_len, ref_count)
    mixed = call(
        functools.partial(attention, plan),
        like(shards, rows + half + 2 * text_rows, HD),
        [SMEM] * 4 + [VMEM] * 5,
        VMEM,
        [
            pltpu.VMEM((2, plan.images, HD), dtype),
            pltpu.VMEM((2, plan.images, 2 * HD), dtype),
            pltpu.VMEM((6, plan.slots, HD), dtype),
            pltpu.VMEM((2, plan.slots, 2 * HD), dtype),
        ],
    )(place, *lengths, whole, *parts)
    returned = lax.all_to_all(mixed, "sp", split_axis=0, concat_axis=0, tiled=True)
    image_out, text_out = call(
        functools.partial(unpack, plan),
        (like(rows, width), like(text_rows, width)),
        [SMEM] * 4 + [VMEM],
        (VMEM, VMEM),
    )(place, *lengths, returned)
    return (image_out[None], text_out[None])


def solution(mesh):
    spec = P("grp", "sp", None)
    return jax.shard_map(
        on_device,
        mesh=mesh,
        in_specs=(spec, spec, spec, spec, P(), P(), P()),
        out_specs=(spec, spec),
        check_vma=False,
    )
```

```python
import functools
import math

import jax
import jax.numpy as jnp
from jax import lax
from jax.experimental import pallas as pl
from jax.experimental.pallas import tpu as pltpu
from jax.sharding import PartitionSpec as P

HD = 128
SIDE = 4
EARLY = 3
NEG_FILL = -1e30
FLOPS_S = 30000000000
FACTOR = math.log2(math.e) / math.sqrt(HD)
VMEM_LIMIT = 48 * 1024 * 1024
VMEM = pl.BlockSpec(memory_space=pltpu.VMEM)
SMEM = pl.BlockSpec(memory_space=pltpu.SMEM)


def call(body, out_shape, in_specs, out_specs, scratch_shapes=(), grid=(), cost=None, aliases={}):
    return pl.pallas_call(
        body,
        grid=grid,
        cost_estimate=cost,
        input_output_aliases=aliases,
        out_shape=out_shape,
        in_specs=in_specs,
        out_specs=out_specs,
        scratch_shapes=list(scratch_shapes),
        compiler_params=pltpu.CompilerParams(vmem_limit_bytes=VMEM_LIMIT),
    )


class Plan:
    def __init__(self, groups, shards, rows, text_rows, width):
        self.groups = groups
        self.shards = shards
        self.rows = rows
        self.half = rows // 2
        self.text_rows = text_rows
        self.heads = width // HD
        self.slots = shards * text_rows
        self.images = shards * rows

    def side(self, device):
        return (device // SIDE) % 2

    def shared(self, device):
        return self.shards + (device // SIDE // 2) * SIDE + device % SIDE


def head(column):
    return slice(column * HD, (column + 1) * HD)


def head_at(column):
    return pl.ds(pl.multiple_of(column * HD, HD), HD)


def step_to(place, dy, dz):
    return lax.rem(place[1] + dy, SIDE), lax.rem(place[2] + dz, SIDE)


def step_from(place, dy, dz):
    y, z = step_to(place, SIDE - dy, SIDE - dz)
    return y * SIDE + z


def pack_shared(plan, place, q, k, v, *outs):
    rows = plan.rows
    for dz in range(SIDE):
        z = lax.rem(place[2] + dz, SIDE)
        for pair in range(2):
            for part, ref in enumerate((q, k, v)):
                outs[dz][pair, part * rows : (part + 1) * rows, :] = ref[:, head_at(plan.shards + pair * SIDE + z)]


def pack_whole(plan, q, k, v, out):
    rows = plan.rows
    for device in range(plan.shards):
        for part, ref in enumerate((q, k, v)):
            out[device, part * rows : (part + 1) * rows, :] = ref[:, head(device)]


def pack_text(plan, place, assign, h0, h2, h4, h6, early, also, whole, out):
    owner = jnp.int32(0)
    for request in range(1, plan.groups):
        owner = jnp.where(assign[request] == place[0], request, owner)
    came = lax.rem(lax.div(lax.bitwise_xor(owner, place[0]), 2), 4)
    for turn, ref in enumerate((h0, h2, h4, h6)):

        @pl.when(came == turn)
        def _(ref=ref):
            for device in range(plan.shards):
                both = (device, plan.shared(device))
                pieces = [ref[:, head(part * plan.heads + own)].astype(jnp.float32) for own in both for part in range(3)]
                out[device, :, :] = jnp.concatenate(pieces, axis=0).astype(jnp.bfloat16)


def choose(place, assign, h0, h8, h1, h9, *outs):
    group = place[0]
    for turn, out in zip((0, 2, 4, 6), outs):
        target = lax.bitwise_xor(group, turn)
        out[...] = h0[...]
        for bits, ref in ((1, h1), (8, h8), (9, h9)):

            @pl.when(assign[lax.bitwise_xor(group, bits)] == target)
            def _(ref=ref, out=out):
                out[...] = ref[...]


def regroup_shared(plan, place, *refs):
    rows, half = plan.rows, plan.half
    ins, outs = refs[:SIDE], refs[SIDE:]
    for dy in range(SIDE):
        y = lax.rem(place[1] + dy, SIDE)
        pair, side = lax.div(y, 2), lax.rem(y, 2)
        mine = pl.ds(pl.multiple_of(side * half, half), half)
        for dz in range(SIDE):
            outs[dy][dz, 0:half, :] = ins[dz][pair, mine, :]
            outs[dy][dz, half:, :] = ins[dz][pair, rows:, :]


def owner_counts(plan, place, assign, prompt_len, ref_count):
    prompt, ref = prompt_len[0], ref_count[0]
    for request in range(1, plan.groups):
        here = assign[request] == place[0]
        prompt = jnp.where(here, prompt_len[request], prompt)
        ref = jnp.where(here, ref_count[request], ref)
    return prompt, ref


def is_alive(plan, slot, counts):
    prompt, ref = counts
    ref_slots = plan.slots - plan.slots // 2
    return slot < jnp.where(slot < ref_slots, ref, ref_slots + prompt)


def scores(queries, keys):
    return lax.dot_general(queries, keys, (((1,), (1,)), ((), ())), preferred_element_type=jnp.float32)


def weights(score, top):
    return jnp.exp2((score - top) * FACTOR).astype(jnp.bfloat16)


def largest(score):
    return jnp.max(score, axis=1, keepdims=True)


def total(weight, values):
    return jnp.dot(weight, values, preferred_element_type=jnp.float32)


def attend(queries, pieces):
    parts = [scores(queries, keys) for keys, _, _ in pieces]
    parts = [part if alive is None else jnp.where(alive, part, NEG_FILL) for part, (_, _, alive) in zip(parts, pieces)]
    top = functools.reduce(jnp.maximum, [largest(part) for part in parts])
    mixed = sum(total(weights(part, top), values) for part, (_, values, _) in zip(parts, pieces))
    return (mixed[:, :HD] / mixed[:, HD:]).astype(jnp.bfloat16)


def attention(plan, place, assign, prompt_len, ref_count, came, p0, p1, p2, p3, out, texts):
    rows, half, text_rows, slots = plan.rows, plan.half, plan.text_rows, plan.slots
    alive = is_alive(plan, lax.broadcasted_iota(jnp.int32, (1, slots), 1), owner_counts(plan, place, assign, prompt_len, ref_count))
    parts = (p0, p1, p2, p3)
    for source in range(0, plan.shards, 2):
        pair = [came[source + i, 3 * rows :, :].astype(jnp.float32) for i in range(2)]
        at = source * text_rows
        for kind in range(6):
            cut = slice(kind * text_rows, (kind + 1) * text_rows)
            texts[kind, at : at + 2 * text_rows, :] = jnp.concatenate([one[cut] for one in pair], axis=0).astype(jnp.bfloat16)

    def with_ones(values):
        return jnp.concatenate([values, jnp.ones_like(values)], axis=1)

    def pieces(which):
        for block in range(SIDE):
            if which == 0:
                mine, at = came.at[block * SIDE : (block + 1) * SIDE], rows
            else:
                mine, at = parts[block], half
            keys = mine[:, at : at + rows, :].reshape(SIDE * rows, HD)
            values = mine[:, at + rows : at + 2 * rows, :].reshape(SIDE * rows, HD)
            yield keys, with_ones(values), None
        yield texts[3 * which + 1], with_ones(texts[3 * which + 2]), alive

    def mix(which, queries):
        return attend(queries, list(pieces(which)))

    for source in range(0, plan.shards, 2):
        mixed = mix(0, came[source : source + 2, 0:rows, :].reshape(2 * rows, HD))
        out[source : source + 2, 0:rows, :] = mixed.reshape(2, rows, HD)
    for dy in range(SIDE):
        mixed = mix(1, parts[dy][:, 0:half, :].reshape(SIDE * half, HD))
        for dz in range(SIDE):
            out[step_from(place, dy, dz), rows : rows + half, :] = mixed[dz * half : (dz + 1) * half]
    own_text, other_text = (mix(which, texts[3 * which]).astype(jnp.float32) for which in range(2))
    for source in range(plan.shards):
        cut = slice(source * text_rows, (source + 1) * text_rows)
        out[source, rows + half :, :] = jnp.concatenate([own_text[cut], other_text[cut]], axis=0).astype(jnp.bfloat16)


def unpack(plan, place, assign, prompt_len, ref_count, returned, image_out, text_out):
    rows, half, text_rows = plan.rows, plan.half, plan.text_rows
    slot = (place[1] * SIDE + place[2]) * text_rows + lax.broadcasted_iota(jnp.int32, (text_rows, 1), 0)
    alive = is_alive(plan, slot, owner_counts(plan, place, assign, prompt_len, ref_count))
    for device in range(plan.shards):
        side, shared = plan.side(device), plan.shared(device)
        image_out[:, head(device)] = returned[device, 0:rows, :]
        image_out[side * half : (side + 1) * half, head(shared)] = returned[device, rows : rows + half, :]
        text = returned[device, rows + half :, :].astype(jnp.float32)
        text_out[:, head(device)] = jnp.where(alive, text[:text_rows], 0.0).astype(text_out.dtype)
        if side == 0:
            text_out[:, head(shared)] = jnp.where(alive, text[text_rows:], 0.0).astype(text_out.dtype)


def route(plan, place, assign, rows):
    def exchange(data, bits):
        return lax.ppermute(data, "grp", [(i, i ^ bits) for i in range(plan.groups)])

    held = [rows] + [exchange(rows, bits) for bits in (8, 1, 9)]
    shape = jax.ShapeDtypeStruct(rows.shape, rows.dtype)
    bound = call(choose, (shape,) * 4, [SMEM] * 2 + [VMEM] * 4, (VMEM,) * 4)(place, assign, *held)
    return [bound[0]] + [exchange(packet, bits) for packet, bits in zip(bound[1:], (2, 4, 6))]


def shift(data, dy, dz, shards):
    pairs = [(i, (i // SIDE + dy) % SIDE * SIDE + (i + dz) % SIDE) for i in range(shards)]
    return lax.ppermute(data, "sp", pairs)


def along_z(parts, shards):
    return [parts[0]] + [shift(parts[dz], 0, dz, shards) for dz in range(1, SIDE)]


def along_y(parts, shards):
    return [parts[0]] + [shift(parts[dy], dy, 0, shards) for dy in range(1, SIDE)]


def on_device(img_q, img_k, img_v, cond_rows, prompt_len, ref_count, assign):
    group = lax.axis_index("grp")
    shard = lax.axis_index("sp")
    groups = lax.axis_size("grp")
    shards = lax.axis_size("sp")
    _, rows, width = img_q.shape
    text_rows = cond_rows.shape[1]
    half = rows // 2
    plan = Plan(groups, shards, rows, text_rows, width)
    place = jnp.stack([group, shard // SIDE, shard % SIDE]).astype(jnp.int32)
    dtype = img_q.dtype

    def like(*shape, dtype=dtype):
        return jax.ShapeDtypeStruct(shape, dtype)

    images = (img_q[0], img_k[0], img_v[0])
    parts = call(
        functools.partial(pack_shared, plan),
        (like(2, 3 * rows, HD),) * SIDE,
        [SMEM] + [VMEM] * 3,
        (VMEM,) * SIDE,
    )(place, *images)
    parts = along_z(parts, shards)
    early = (parts[1], parts[EARLY])
    parts = call(
        functools.partial(regroup_shared, plan),
        (like(SIDE, half + 2 * rows, HD),) * SIDE,
        [SMEM] + [VMEM] * SIDE,
        (VMEM,) * SIDE,
        cost=pl.CostEstimate(flops=FLOPS_S, transcendentals=0, bytes_accessed=0),
    )(place, *parts)
    parts = along_y(parts, shards)

    texts = route(plan, place, assign, cond_rows[0])
    block = (shards, 3 * rows, HD)
    shape = like(shards, 3 * rows + 6 * text_rows, HD)
    whole = call(
        functools.partial(pack_whole, plan),
        shape,
        [pl.BlockSpec((rows, width), lambda i: (0, 0))] * 3,
        pl.BlockSpec(block, lambda i: (0, 0, 0)),
        grid=(1,),
    )(*images)
    anywhere = pl.BlockSpec(memory_space=pl.ANY)
    packet = pl.BlockSpec((text_rows, 3 * width), lambda i: (0, 0))
    whole = call(
        functools.partial(pack_text, plan),
        shape,
        [SMEM] * 2 + [packet] * SIDE + [anywhere] * 3,
        pl.BlockSpec((shards, 6 * text_rows, HD), lambda i: (0, 3 * rows // (6 * text_rows), 0)),
        grid=(1,),
        aliases={8: 0},
    )(place, assign, *texts, *early, whole)
    whole = lax.all_to_all(whole, "sp", split_axis=0, concat_axis=0, tiled=True)

    lengths = (assign, prompt_len, ref_count)
    mixed = call(
        functools.partial(attention, plan),
        like(shards, rows + half + 2 * text_rows, HD),
        [SMEM] * 4 + [VMEM] * 5,
        VMEM,
        [
            pltpu.VMEM((6, plan.slots, HD), dtype),
        ],
    )(place, *lengths, whole, *parts)
    returned = lax.all_to_all(mixed, "sp", split_axis=0, concat_axis=0, tiled=True)
    image_out, text_out = call(
        functools.partial(unpack, plan),
        (like(rows, width), like(text_rows, width)),
        [SMEM] * 4 + [VMEM],
        (VMEM, VMEM),
    )(place, *lengths, returned)
    return (image_out[None], text_out[None])


def solution(mesh):
    spec = P("grp", "sp", None)
    return jax.shard_map(
        on_device,
        mesh=mesh,
        in_specs=(spec, spec, spec, spec, P(), P(), P()),
        out_specs=(spec, spec),
        check_vma=False,
    )
```

```python
import functools
import math

import jax
import jax.numpy as jnp
from jax import lax
from jax.experimental import pallas as pl
from jax.experimental.pallas import tpu as pltpu
from jax.sharding import PartitionSpec as P

HD = 128
SIDE = 4
EARLY = 3
NEG_FILL = -1e30
FLOPS_S = 30000000000
FACTOR = math.log2(math.e) / math.sqrt(HD)
VMEM_LIMIT = 48 * 1024 * 1024
VMEM = pl.BlockSpec(memory_space=pltpu.VMEM)
SMEM = pl.BlockSpec(memory_space=pltpu.SMEM)


def call(body, out_shape, in_specs, out_specs, scratch_shapes=(), grid=(), cost=None, aliases={}):
    return pl.pallas_call(
        body,
        grid=grid,
        cost_estimate=cost,
        input_output_aliases=aliases,
        out_shape=out_shape,
        in_specs=in_specs,
        out_specs=out_specs,
        scratch_shapes=list(scratch_shapes),
        compiler_params=pltpu.CompilerParams(vmem_limit_bytes=VMEM_LIMIT),
    )


class Plan:
    def __init__(self, groups, shards, rows, text_rows, width):
        self.groups = groups
        self.shards = shards
        self.rows = rows
        self.half = rows // 2
        self.text_rows = text_rows
        self.heads = width // HD
        self.slots = shards * text_rows
        self.images = shards * rows

    def side(self, device):
        return (device // SIDE) % 2

    def shared(self, device):
        return self.shards + (device // SIDE // 2) * SIDE + device % SIDE


def head(column):
    return slice(column * HD, (column + 1) * HD)


def head_at(column):
    return pl.ds(pl.multiple_of(column * HD, HD), HD)


def step_to(place, dy, dz):
    return lax.rem(place[1] + dy, SIDE), lax.rem(place[2] + dz, SIDE)


def step_from(place, dy, dz):
    y, z = step_to(place, SIDE - dy, SIDE - dz)
    return y * SIDE + z


def pack_shared(plan, place, q, k, v, *outs):
    rows = plan.rows
    for dz in range(SIDE):
        z = lax.rem(place[2] + dz, SIDE)
        for pair in range(2):
            for part, ref in enumerate((q, k, v)):
                outs[dz][pair, part * rows : (part + 1) * rows, :] = ref[:, head_at(plan.shards + pair * SIDE + z)]


def pack_whole(plan, q, k, v, out):
    rows = plan.rows
    for device in range(plan.shards):
        for part, ref in enumerate((q, k, v)):
            out[device, part * rows : (part + 1) * rows, :] = ref[:, head(device)]


def pack_text(plan, place, assign, h0, h2, h4, h6, early, also, whole, out):
    owner = jnp.int32(0)
    for request in range(1, plan.groups):
        owner = jnp.where(assign[request] == place[0], request, owner)
    came = lax.rem(lax.div(lax.bitwise_xor(owner, place[0]), 2), 4)
    for turn, ref in enumerate((h0, h2, h4, h6)):

        @pl.when(came == turn)
        def _(ref=ref):
            for device in range(plan.shards):
                both = (device, plan.shared(device))
                pieces = [ref[:, head(part * plan.heads + own)].astype(jnp.float32) for own in both for part in range(3)]
                out[device, :, :] = jnp.concatenate(pieces, axis=0).astype(jnp.bfloat16)


def choose(place, assign, h0, h8, h1, h9, *outs):
    group = place[0]
    for turn, out in zip((0, 2, 4, 6), outs):
        target = lax.bitwise_xor(group, turn)
        out[...] = h0[...]
        for bits, ref in ((1, h1), (8, h8), (9, h9)):

            @pl.when(assign[lax.bitwise_xor(group, bits)] == target)
            def _(ref=ref, out=out):
                out[...] = ref[...]


def regroup_shared(plan, place, *refs):
    rows, half = plan.rows, plan.half
    ins, outs = refs[:SIDE], refs[SIDE:]
    for dy in range(SIDE):
        y = lax.rem(place[1] + dy, SIDE)
        pair, side = lax.div(y, 2), lax.rem(y, 2)
        mine = pl.ds(pl.multiple_of(side * half, half), half)
        for dz in range(SIDE):
            outs[dy][dz, 0:half, :] = ins[dz][pair, mine, :]
            outs[dy][dz, half:, :] = ins[dz][pair, rows:, :]


def owner_counts(plan, place, assign, prompt_len, ref_count):
    prompt, ref = prompt_len[0], ref_count[0]
    for request in range(1, plan.groups):
        here = assign[request] == place[0]
        prompt = jnp.where(here, prompt_len[request], prompt)
        ref = jnp.where(here, ref_count[request], ref)
    return prompt, ref


def is_alive(plan, slot, counts):
    prompt, ref = counts
    ref_slots = plan.slots - plan.slots // 2
    return slot < jnp.where(slot < ref_slots, ref, ref_slots + prompt)


def scores(queries, keys):
    return lax.dot_general(queries, keys, (((1,), (1,)), ((), ())), preferred_element_type=jnp.float32)


def weights(score, top):
    return jnp.exp2((score - top) * FACTOR).astype(jnp.bfloat16)


def largest(score):
    return jnp.max(score, axis=1, keepdims=True)


def total(weight, values):
    return jnp.dot(weight, values, preferred_element_type=jnp.float32)


def attend(queries, pieces):
    parts = [scores(queries, keys) for keys, _, _ in pieces]
    parts = [part if alive is None else jnp.where(alive, part, NEG_FILL) for part, (_, _, alive) in zip(parts, pieces)]
    top = functools.reduce(jnp.maximum, [largest(part) for part in parts])
    mixed = sum(total(weights(part, top), values) for part, (_, values, _) in zip(parts, pieces))
    return (mixed[:, :HD] / mixed[:, HD:]).astype(jnp.bfloat16)


def attention(plan, place, assign, prompt_len, ref_count, came, p0, p1, p2, p3, out, texts):
    rows, half, text_rows, slots = plan.rows, plan.half, plan.text_rows, plan.slots
    alive = is_alive(plan, lax.broadcasted_iota(jnp.int32, (1, slots), 1), owner_counts(plan, place, assign, prompt_len, ref_count))
    parts = (p0, p1, p2, p3)
    for source in range(0, plan.shards, 2):
        pair = [came[source + i, 3 * rows :, :].astype(jnp.float32) for i in range(2)]
        at = source * text_rows
        for kind in range(6):
            cut = slice(kind * text_rows, (kind + 1) * text_rows)
            texts[kind, at : at + 2 * text_rows, :] = jnp.concatenate([one[cut] for one in pair], axis=0).astype(jnp.bfloat16)

    def with_ones(values):
        return jnp.concatenate([values, jnp.ones_like(values)], axis=1)

    def pieces(which):
        for block in range(SIDE):
            if which == 0:
                mine, at = came.at[block * SIDE : (block + 1) * SIDE], rows
            else:
                mine, at = parts[block], half
            keys = mine[:, at : at + rows, :].reshape(SIDE * rows, HD)
            values = mine[:, at + rows : at + 2 * rows, :].reshape(SIDE * rows, HD)
            yield keys, with_ones(values), None
        yield texts[3 * which + 1], with_ones(texts[3 * which + 2]), alive

    def mix(which, queries):
        return attend(queries, list(pieces(which)))

    for source in range(0, plan.shards, 2):
        mixed = mix(0, came[source : source + 2, 0:rows, :].reshape(2 * rows, HD))
        out[source : source + 2, 0:rows, :] = mixed.reshape(2, rows, HD)
    for dy in range(SIDE):
        mixed = mix(1, parts[dy][:, 0:half, :].reshape(SIDE * half, HD))
        for dz in range(SIDE):
            out[step_from(place, dy, dz), rows : rows + half, :] = mixed[dz * half : (dz + 1) * half]
    own_text, other_text = (mix(which, texts[3 * which]).astype(jnp.float32) for which in range(2))
    for source in range(plan.shards):
        cut = slice(source * text_rows, (source + 1) * text_rows)
        out[source, rows + half :, :] = jnp.concatenate([own_text[cut], other_text[cut]], axis=0).astype(jnp.bfloat16)


def unpack(plan, place, assign, prompt_len, ref_count, returned, image_out, text_out):
    rows, half, text_rows = plan.rows, plan.half, plan.text_rows
    slot = (place[1] * SIDE + place[2]) * text_rows + lax.broadcasted_iota(jnp.int32, (text_rows, 1), 0)
    alive = is_alive(plan, slot, owner_counts(plan, place, assign, prompt_len, ref_count))
    step = pl.program_id(0)
    per = plan.shards // 2

    def put(column, first, at):
        text_out[:, head(column)] = jnp.where(alive, first[at : at + text_rows].astype(jnp.float32), 0.0).astype(text_out.dtype)

    @pl.when(step < 2)
    def _():
        for i in range(per):
            device = step * per + i
            image_out[:, head(i)] = returned[device, 0:rows, :]
            put(i, returned[device, rows + half :, :].astype(jnp.float32), 0)

    @pl.when(step == 2)
    def _():
        for device in range(plan.shards):
            side, column = plan.side(device), plan.shared(device) - plan.shards
            image_out[side * half : (side + 1) * half, head(column)] = returned[device, rows : rows + half, :]
            if side == 0:
                put(column, returned[device, rows + half :, :].astype(jnp.float32), text_rows)


def route(plan, place, assign, rows):
    def exchange(data, bits):
        return lax.ppermute(data, "grp", [(i, i ^ bits) for i in range(plan.groups)])

    held = [rows] + [exchange(rows, bits) for bits in (8, 1, 9)]
    shape = jax.ShapeDtypeStruct(rows.shape, rows.dtype)
    bound = call(choose, (shape,) * 4, [SMEM] * 2 + [VMEM] * 4, (VMEM,) * 4)(place, assign, *held)
    return [bound[0]] + [exchange(packet, bits) for packet, bits in zip(bound[1:], (2, 4, 6))]


def shift(data, dy, dz, shards):
    pairs = [(i, (i // SIDE + dy) % SIDE * SIDE + (i + dz) % SIDE) for i in range(shards)]
    return lax.ppermute(data, "sp", pairs)


def along_z(parts, shards):
    return [parts[0]] + [shift(parts[dz], 0, dz, shards) for dz in range(1, SIDE)]


def along_y(parts, shards):
    return [parts[0]] + [shift(parts[dy], dy, 0, shards) for dy in range(1, SIDE)]


def on_device(img_q, img_k, img_v, cond_rows, prompt_len, ref_count, assign):
    group = lax.axis_index("grp")
    shard = lax.axis_index("sp")
    groups = lax.axis_size("grp")
    shards = lax.axis_size("sp")
    _, rows, width = img_q.shape
    text_rows = cond_rows.shape[1]
    half = rows // 2
    plan = Plan(groups, shards, rows, text_rows, width)
    place = jnp.stack([group, shard // SIDE, shard % SIDE]).astype(jnp.int32)
    dtype = img_q.dtype

    def like(*shape, dtype=dtype):
        return jax.ShapeDtypeStruct(shape, dtype)

    images = (img_q[0], img_k[0], img_v[0])
    parts = call(
        functools.partial(pack_shared, plan),
        (like(2, 3 * rows, HD),) * SIDE,
        [SMEM] + [VMEM] * 3,
        (VMEM,) * SIDE,
    )(place, *images)
    parts = along_z(parts, shards)
    early = (parts[1], parts[EARLY])
    parts = call(
        functools.partial(regroup_shared, plan),
        (like(SIDE, half + 2 * rows, HD),) * SIDE,
        [SMEM] + [VMEM] * SIDE,
        (VMEM,) * SIDE,
        cost=pl.CostEstimate(flops=FLOPS_S, transcendentals=0, bytes_accessed=0),
    )(place, *parts)
    parts = along_y(parts, shards)

    texts = route(plan, place, assign, cond_rows[0])
    block = (shards, 3 * rows, HD)
    shape = like(shards, 3 * rows + 6 * text_rows, HD)
    whole = call(
        functools.partial(pack_whole, plan),
        shape,
        [pl.BlockSpec((rows, width), lambda i: (0, 0))] * 3,
        pl.BlockSpec(block, lambda i: (0, 0, 0)),
        grid=(1,),
    )(*images)
    anywhere = pl.BlockSpec(memory_space=pl.ANY)
    packet = pl.BlockSpec((text_rows, 3 * width), lambda i: (0, 0))
    whole = call(
        functools.partial(pack_text, plan),
        shape,
        [SMEM] * 2 + [packet] * SIDE + [anywhere] * 3,
        pl.BlockSpec((shards, 6 * text_rows, HD), lambda i: (0, 3 * rows // (6 * text_rows), 0)),
        grid=(1,),
        aliases={8: 0},
    )(place, assign, *texts, *early, whole)
    whole = lax.all_to_all(whole, "sp", split_axis=0, concat_axis=0, tiled=True)

    lengths = (assign, prompt_len, ref_count)
    mixed = call(
        functools.partial(attention, plan),
        like(shards, rows + half + 2 * text_rows, HD),
        [SMEM] * 4 + [VMEM] * 5,
        VMEM,
        [
            pltpu.VMEM((6, plan.slots, HD), dtype),
        ],
    )(place, *lengths, whole, *parts)
    returned = lax.all_to_all(mixed, "sp", split_axis=0, concat_axis=0, tiled=True)
    image_out, text_out = call(
        functools.partial(unpack, plan),
        (like(rows, width), like(text_rows, width)),
        [SMEM] * 4 + [VMEM],
        (
            pl.BlockSpec((rows, width // 3), lambda i: (0, i)),
            pl.BlockSpec((text_rows, width // 3), lambda i: (0, i)),
        ),
        grid=(3,),
    )(place, *lengths, returned)
    return (image_out[None], text_out[None])


def solution(mesh):
    spec = P("grp", "sp", None)
    return jax.shard_map(
        on_device,
        mesh=mesh,
        in_specs=(spec, spec, spec, spec, P(), P(), P()),
        out_specs=(spec, spec),
        check_vma=False,
    )
```
